256 devices in a mesh: visit: 64 (over z, x, core), band: 4 (over y).
Axes of the slice: x: 4, y: 4, z: 8, core: 2. Of those that a mesh axis runs over, the one named last changes fastest.
Arguments:
- images: float32 [4, 32768, 2048], P('band', 'visit'), may hold values from -12 to 12
- row_kernel: float32 [4, 64, 31], P('band', 'visit'), may hold values from 0.05 to 0.4
- col_kernel: float32 [4, 64, 31], P('band', 'visit'), may hold values from 0.05 to 0.4
- patch_ids: int32 [4, 2048, 2], P('band', 'visit'), may hold values from 0 to 63, all different within a row; in each aligned block of 32 rows (0 to 31, 32 to 63, ..., all dimensions but the last counted through in order) at most 2 rows name the same one
- row_offsets: int32 [4, 2048, 2], P('band', 'visit'), may hold values from 0 to 32
- weight_codes: int32 [4, 2048, 2], P('band', 'visit'), may hold values from 1 to 15
- detect_row_taps: float32 [4, 9], replicated, may hold values from 0.1 to 0.6
- detect_col_taps: float32 [4, 9], replicated, may hold values from 0.1 to 0.6
- band_weights: float32 [4], replicated, may hold values from 0.3 to 1
Outputs:
- coadd_image: float32 [4, 3072, 2048], P('band', 'visit')
- detection: float32 [3072, 2048], P(('visit', 'band'))
The draws below stay inside these ranges and needn't reach their ends.
Inputs may be any that keep to these rules, and one draw needn't show every extreme that they name: `patch_ids`: each block names 2 different patches; among the blocks of one exposure no patch is named more than 2 times, and in some exposures one patch is named exactly 2 times.
All inputs are finite; a program needn't handle non-finite values.
Results may differ from the reference program's by a relative error of at most 0.0001.
Values sent between devices are 32-bit elements; how exact they have to be, the bound alone decides.
A program may use at most 128 MiB of HBM per device.

```python
import math
import jax
import jax.numpy as jnp
import numpy as np
from jax import lax

COLS = 2048
BLOCK_ROWS = 16
BLOCKS_DEV = 32
PATCH_ROWS = 48
TAPS = 31
DETECT_TAPS = 9
INTERSECTIONS = 2
ROWS_DEV = 512
PATCHES = 64
BANDS = 4
CAPACITY = 2
N_VISIT = 64


def with_ends(array, stream_key, smallest, largest):
    place = [jax.random.randint(jax.random.fold_in(stream_key, axis), (), 0, length) for axis, length in enumerate(array.shape)]
    longest = array.shape.index(max(array.shape))
    next_to = place[:longest] + [(place[longest] + 1) % array.shape[longest]] + place[longest + 1:]
    return array.at[tuple(place)].set(smallest).at[tuple(next_to)].set(largest)


def level_of(key, dims, pieces, low, largest):
    level, own = 1.0, jax.random.fold_in(key, 6)
    for position, shards_of in pieces:
        steps = jnp.exp(jax.random.uniform(jax.random.fold_in(own, position), (shards_of,), jnp.float32, low / len(pieces), largest / len(pieces)))
        level = level * jnp.repeat(steps, dims[position] // shards_of).reshape([-1 if axis == position else 1 for axis in range(len(dims))])
    return level


def shared_out(rng, own, number, rows, count, top, limit, lean):
    order = jax.random.permutation(rng, count)
    packed, common = shares(count, rows * top, limit, lean, True), shares(count, rows * top, limit, lean, False)
    places = jnp.arange(count)

    def named(tallies, offset_by):
        used = int((tallies > 0).sum())
        fixed = max(1, used // 4)
        passed = fixed + (places - fixed + offset_by * (used - fixed)) % max(1, count - fixed)
        return jnp.zeros((count,), jnp.int32).at[order[jnp.where(places < fixed, places, passed)]].set(jnp.asarray(tallies, jnp.int32))

    tallies = jnp.where(number % 4 == 0, named(packed, number // 4), named(common, number - number // 4 - 1))
    mixed = jax.random.permutation(jax.random.fold_in(own, 3), count)
    source_of, sink = mixed[0:count // 2 * 2:2], mixed[1:count // 2 * 2:2]
    slack = jnp.minimum(tallies[source_of] - 1, limit - tallies[sink]) // 2
    slack = jnp.where((source_of == order[0]) | (sink == order[0]) | (tallies[sink] == 0), 0, jnp.maximum(slack, 0))
    passed = jax.random.randint(jax.random.fold_in(own, 4), (count // 2,), 0, 1 << 20) % (slack + 1)
    tallies = tallies.at[source_of].add(-passed).at[sink].add(passed)
    members = jnp.searchsorted(jnp.cumsum(tallies), jnp.arange(rows * top), side="right").astype(jnp.int32)
    listing = members.reshape(top, rows).T
    listing = listing[jax.random.permutation(jax.random.fold_in(own, 1), rows)]
    offset_by = jax.random.randint(jax.random.fold_in(own, 2), (rows, 1), 0, top)
    return jnp.take_along_axis(listing, (jnp.arange(top)[None, :] + offset_by) % top, axis=1)


def shares(number_of, total, reach, slope, full):
    weights = [(1 << 20) // math.isqrt(rank ** slope) + 1 for rank in range(1, number_of + 1)]
    largest = reach if full else min(reach, max(-(-total // number_of), total * weights[0] // sum(weights)))
    least = 1 if total - largest >= number_of - 1 else 0
    counts, surplus = [largest] + [least] * (number_of - 1), total - largest - least * (number_of - 1)
    while surplus > 0:
        movable = [i for i in range(1, number_of) if counts[i] < largest] or [i for i in range(1, number_of) if counts[i] < reach]
        mass, left = sum([weights[i] for i in movable]), surplus
        for i in movable:
            more = min(reach - counts[i], max(1, left * weights[i] // mass), surplus)
            counts[i] = counts[i] + more
            surplus = surplus - more
    return np.array(counts)


def normal_values(own_key, dims, deviation, reach, shards=(), held_as=jnp.bfloat16):
    level = level_of(own_key, dims, shards, -0.22, 0.18) if shards else 1.0
    result = jax.random.normal(own_key, dims, jnp.float32) * deviation * level
    return jnp.minimum(jnp.maximum(result, -reach), reach).astype(held_as)


def setup_inputs(seed: int = 0) -> dict:
    splits = jax.random.split(jax.random.key(seed), 10)
    images = normal_values(splits[0], (BANDS, N_VISIT * ROWS_DEV, COLS), 2.0, 12.0, ((0, 4), (1, 64)), jnp.float32)
    row_kernel = jnp.clip(jnp.exp(math.log(0.4) - 2.0794415 * jax.random.uniform(splits[1], (BANDS, N_VISIT, TAPS), jnp.float32) ** level_of(splits[1], (BANDS, N_VISIT, TAPS), ((0, 4), (1, 64)), -0.2, 0.2)), 0.05, 0.4)
    col_kernel = jnp.clip(jnp.exp(math.log(0.4) - 2.0794415 * jax.random.uniform(splits[2], (BANDS, N_VISIT, TAPS), jnp.float32) ** level_of(splits[2], (BANDS, N_VISIT, TAPS), ((0, 4), (1, 64)), -0.2, 0.2)), 0.05, 0.4)
    patch_ids_keys = jax.random.split(jax.random.fold_in(splits[3], 1), BANDS * (N_VISIT * BLOCKS_DEV) // BLOCKS_DEV)
    patch_ids_turns = jax.random.permutation(jax.random.fold_in(splits[3], 3), BANDS * (N_VISIT * BLOCKS_DEV) // BLOCKS_DEV)
    patch_ids = jax.vmap(lambda own, number: shared_out(jax.random.fold_in(splits[3], 2), own, number, BLOCKS_DEV, PATCHES, INTERSECTIONS, CAPACITY, 2))(patch_ids_keys, patch_ids_turns).reshape((BANDS, N_VISIT * BLOCKS_DEV, INTERSECTIONS))
    row_offsets = with_ends(jax.random.randint(splits[4], (BANDS, N_VISIT * BLOCKS_DEV, INTERSECTIONS), 0, PATCH_ROWS - BLOCK_ROWS + 1), jax.random.fold_in(splits[4], 1), 0, PATCH_ROWS - BLOCK_ROWS).astype(jnp.int32)
    weight_codes = with_ends(jax.random.randint(splits[5], (BANDS, N_VISIT * BLOCKS_DEV, INTERSECTIONS), 1, 16), jax.random.fold_in(splits[5], 1), 1, 15).astype(jnp.int32)
    detect_row_taps = jnp.clip(jnp.exp(jax.random.uniform(splits[6], (BANDS, DETECT_TAPS), jnp.float32, math.log(0.1), math.log(0.6))), 0.1, 0.6)
    detect_col_taps = jnp.clip(jnp.exp(jax.random.uniform(splits[7], (BANDS, DETECT_TAPS), jnp.float32, math.log(0.1), math.log(0.6))), 0.1, 0.6)
    band_weights = jnp.clip(jnp.exp(jax.random.uniform(splits[8], (BANDS,), jnp.float32, math.log(0.3), math.log(1.0))), 0.3, 1.0)
    return dict(images=images, row_kernel=row_kernel, col_kernel=col_kernel, patch_ids=patch_ids, row_offsets=row_offsets, weight_codes=weight_codes, detect_row_taps=detect_row_taps, detect_col_taps=detect_col_taps, band_weights=band_weights)


def correlate(values, kernel, axis_dim):
    tap_count = kernel.shape[-1]
    half_width = (tap_count - 1) // 2
    widths = [(0, 0)] * values.ndim
    widths[axis_dim] = (half_width, half_width)
    padded = jnp.pad(values, widths)
    length = values.shape[axis_dim]
    accumulated = jnp.zeros(values.shape, jnp.float32)
    for tap_index in range(tap_count):
        accumulated = accumulated + kernel[..., tap_index] * lax.slice_in_dim(padded, tap_index, tap_index + length, axis=axis_dim)
    return accumulated


def reference(images, row_kernel, col_kernel, patch_ids, row_offsets, weight_codes, detect_row_taps, detect_col_taps, band_weights):
    coadds = []
    inner_rows = jnp.arange(BLOCK_ROWS, dtype=jnp.int32)
    for band_index in range(BANDS):
        strips = images[band_index].reshape(N_VISIT, ROWS_DEV, COLS)
        row_taps = row_kernel[band_index][:, None, None, :]
        col_taps = col_kernel[band_index][:, None, None, :]
        matched = correlate(correlate(strips, row_taps, 1), col_taps, 2)
        blocks = matched.reshape(N_VISIT * BLOCKS_DEV, BLOCK_ROWS, COLS)
        numerator = jnp.zeros((PATCHES * PATCH_ROWS, COLS), jnp.float32)
        weight_sum = jnp.zeros((PATCHES * PATCH_ROWS,), jnp.float32)
        for route_slot in range(INTERSECTIONS):
            first_rows = (patch_ids[band_index, :, route_slot] * PATCH_ROWS + row_offsets[band_index, :, route_slot]).astype(jnp.int32)
            row_index = first_rows[:, None] + inner_rows[None, :]
            weights = weight_codes[band_index, :, route_slot].astype(jnp.float32)
            numerator = numerator.at[row_index].add(weights[:, None, None] * blocks)
            weight_sum = weight_sum.at[row_index].add(jnp.broadcast_to(weights[:, None], row_index.shape))
        coadds.append(numerator / (1.0 + weight_sum)[:, None])
    coadd_image = jnp.stack(coadds, 0)
    detection = jnp.zeros((PATCHES * PATCH_ROWS, COLS), jnp.float32)
    for band_index in range(BANDS):
        patches = coadd_image[band_index].reshape(PATCHES, PATCH_ROWS, COLS)
        row_taps = detect_row_taps[band_index].reshape(1, 1, DETECT_TAPS)
        col_taps = detect_col_taps[band_index].reshape(1, 1, DETECT_TAPS)
        smoothed = correlate(correlate(patches, row_taps, 1), col_taps, 2)
        detection = detection + band_weights[band_index] * smoothed.reshape(PATCHES * PATCH_ROWS, COLS)
    return coadd_image, detection
```

```python
import jax
import jax.numpy as jnp
from jax import lax
from jax.experimental import pallas as pl
from jax.experimental.pallas import tpu as pltpu
from jax.sharding import PartitionSpec as P

MESH = pl.DeviceIdType.MESH
F32, BF16 = jnp.float32, jnp.bfloat16

COLS = 2048
BLOCK_ROWS = 16
BLOCKS = 32
PATCH = 48
TAPS = 31
HALF = 15
DTAPS = 9
DHALF = 4
ROWS = 512
NX, NZ, NB = 4, 8, 4
TILE = 256
NT = COLS // TILE
NP = NT // 2
PAD = 128
GROUP = NZ * PATCH
OWN = NX * GROUP
XROWS = (32, 24)
XCUT = (16, 16)
ZCUT = (8, 16)
SLAB = 12
LAST_AGE = 8


def split(value):
    high = value.astype(BF16)
    return high, (value - high.astype(F32)).astype(BF16)


def dot(a, b):
    return jnp.dot(a, b, preferred_element_type=F32)


def dot3(a_high, a_low, b_high, b_low):
    return dot(a_high, b_high) + dot(a_low, b_high) + dot(a_high, b_low)


def band_block(taps, shift):
    diff = (
        lax.broadcasted_iota(jnp.int32, (128, 128), 0)
        - lax.broadcasted_iota(jnp.int32, (128, 128), 1)
        + shift
    )
    block = jnp.zeros((128, 128), F32)
    for index, tap in enumerate(taps):
        block = jnp.where(diff == index, tap, block)
    return block


def kernel(
    img, rk, ck, pid, off, code, drt, dct, bw,
    coadd_ref, det_ref,
    ximg, xh, xl, trh, trl, tch, tcl, dch, dcl, tdh, tdl,
    meta, meta_sib, phi, mown, msib, mh, ml,
    px0, px1, pz0, pz1, xrx0, xrx1, xrz0, xrz1, zrz0, zrz1, zrx0, zrx1,
    wb, wrx, wz, wrz, inv, rch, rcl, sm, yr,
    img_sem, meta_sem, sib_s, sib_r, s0, s1, r0, r1, w_s, w_r, y_s, y_r,
):
    px, pz = (px0, px1), (pz0, pz1)
    xrx, xrz, zrz, zrx = (xrx0, xrx1), (xrz0, xrz1), (zrz0, zrz1), (zrx0, zrx1)
    ssem, rsem = (s0, s1), (r0, r1)

    v = lax.axis_index("visit")
    b = lax.axis_index("band")
    c = v % 2
    x = (v // 2) % NX
    z = v // (2 * NX)

    def at_x(step):
        return (z * (2 * NX) + ((x + step) % NX) * 2 + c, b)

    def at_z(step):
        return (((z + step) % NZ) * (2 * NX) + x * 2 + c, b)

    def at_y(step):
        return (v, (b + step) % NB)

    sibling = (v + 1 - 2 * c, b)

    def remote(src, dst, send, recv, device):
        return pltpu.make_async_remote_copy(
            src_ref=src, dst_ref=dst, send_sem=send, recv_sem=recv,
            device_id=device, device_id_type=MESH,
        )

    def image_copy(k):
        return pltpu.make_async_copy(
            img.at[0, :, pl.ds(pl.multiple_of(k * TILE, TILE), TILE)], ximg.at[k], img_sem.at[k]
        )

    for k in range(NT):
        image_copy(k).start()

    barrier = pltpu.get_barrier_semaphore()
    partners = (
        [sibling]
        + [at_x(d) for d in range(1, NX)]
        + [at_z(d) for d in range(1, NZ)]
        + [at_y(d) for d in range(1, NB)]
    )
    for partner in partners:
        pl.semaphore_signal(barrier, inc=1, device_id=partner, device_id_type=MESH)

    spread = (
        lax.broadcasted_iota(jnp.int32, (BLOCKS, ROWS), 1) // BLOCK_ROWS
        == lax.broadcasted_iota(jnp.int32, (BLOCKS, ROWS), 0)
    )
    for k, ref in enumerate((pid, off, code)):
        values = ref[0].astype(F32)
        for o in range(2):
            row = jnp.sum(jnp.where(spread, values[:, o : o + 1], 0.0), axis=0, keepdims=True)
            meta[2 * k + o : 2 * k + o + 1, :] = row.astype(jnp.int32)
    meta[6:8, :] = jnp.zeros((2, ROWS), jnp.int32)

    row_taps = [rk[0, 0, m] for m in range(TAPS)]
    col_taps = [ck[0, 0, m] for m in range(TAPS)]
    tch[...] = jnp.zeros(tch.shape, BF16)
    tcl[...] = jnp.zeros(tcl.shape, BF16)
    for d in (-1, 0, 1):
        high, low = split(band_block(col_taps, 128 * d + HALF))
        for cb in range(2):
            ub = d + 1 + cb
            tch[128 * ub : 128 * ub + 128, 128 * cb : 128 * cb + 128] = high
            tcl[128 * ub : 128 * ub + 128, 128 * cb : 128 * cb + 128] = low
    trh[...] = jnp.zeros(trh.shape, BF16)
    trl[...] = jnp.zeros(trl.shape, BF16)
    backward = row_taps[::-1]
    for d in (-1, 0, 1):
        high, low = split(band_block(backward, TAPS - 1 - (128 * d + HALF)))
        for ib in range(4):
            if 0 <= ib + d < 4:
                kb = ib + d
                trh[128 * ib : 128 * ib + 128, 128 * kb : 128 * kb + 128] = high
                trl[128 * ib : 128 * ib + 128, 128 * kb : 128 * kb + 128] = low

    edge = jnp.zeros((ROWS, PAD), BF16)
    for ref in (xh, xl):
        ref[:, 0:PAD] = edge
        ref[:, PAD + COLS : 2 * PAD + COLS] = edge

    def convert(k):
        image_copy(k).wait()
        high, low = split(ximg[k])
        start = pl.multiple_of(PAD + k * TILE, 128)
        xh[:, pl.ds(start, TILE)] = high
        xl[:, pl.ds(start, TILE)] = low

    def sib_copy(j):
        return remote(mown.at[j], msib.at[j], sib_s.at[j], sib_r.at[j], sibling)

    def correlate(j):
        start = pl.multiple_of(j * TILE, TILE)
        window = pl.ds(start, 2 * TILE)
        along = dot3(xh[:, window], xl[:, window], tch[...], tcl[...])
        high, low = split(along)
        mown[j] = dot3(trh[...], trl[...], high, low)
        sib_copy(j).start()

    def targets(source):
        place = lax.broadcasted_iota(jnp.int32, (1, ROWS), 1) % BLOCK_ROWS
        result = []
        for o in range(2):
            ids = source[o : o + 1, :]
            dx = (lax.shift_right_logical(ids, 1) - x) & (NX - 1)
            dz = (lax.shift_right_logical(ids, 3) - z) & (NZ - 1)
            row = (dx * NZ + dz) * PATCH + source[2 + o : 3 + o, :] + place
            result.append(jnp.where((ids & 1) == c, row, -1))
        return result, [source[4 + o : 5 + o, :].astype(F32) for o in range(2)]

    def build_phi(source, first):
        rows, weights = targets(source)
        step = 64

        def body(k, _):
            base = pl.multiple_of(k * step, step)
            index = lax.broadcasted_iota(jnp.int32, (step, ROWS), 0) + base
            value = jnp.where(
                rows[0] == index, weights[0], jnp.where(rows[1] == index, weights[1], 0.0)
            )
            phi[pl.ds(base, step), first : first + ROWS] = value.astype(BF16)
            return 0

        lax.fori_loop(0, OWN // step, body, 0)

    pl.semaphore_wait(barrier, len(partners))
    meta_copy = remote(meta, meta_sib, meta_sem.at[0], meta_sem.at[1], sibling)
    meta_copy.start()
    convert(0)
    convert(1)
    correlate(0)
    build_phi(meta, 0)
    meta_copy.wait_recv()
    build_phi(meta_sib, ROWS)

    dcol_taps = [dct[b, m] for m in range(DTAPS)]
    drow_taps = [bw[b] * drt[b, m] for m in range(DTAPS)]
    dch[...] = jnp.zeros(dch.shape, BF16)
    dcl[...] = jnp.zeros(dcl.shape, BF16)
    for d in (-1, 0, 1):
        high, low = split(band_block(dcol_taps, 128 * d + DHALF))
        for cb in range(2):
            ub = d + 1 + cb
            dch[128 * ub : 128 * ub + 128, 128 * cb : 128 * cb + 128] = high
            dcl[128 * ub : 128 * ub + 128, 128 * cb : 128 * cb + 128] = low
    out_index = lax.broadcasted_iota(jnp.int32, (64, PATCH), 0)
    out_row = SLAB * ((b + out_index // 16) % NB) + out_index % 16
    tap_index = jnp.where(
        out_index % 16 < SLAB,
        lax.broadcasted_iota(jnp.int32, (64, PATCH), 1) - out_row + DHALF,
        -1,
    )
    drow = jnp.zeros((64, PATCH), F32)
    for index, tap in enumerate(drow_taps):
        drow = jnp.where(tap_index == index, tap, drow)
    high, low = split(drow)
    tdh[...] = high
    tdl[...] = low
    slab_edge = jnp.zeros((64, PAD), BF16)
    for ref in (rch, rcl):
        ref[:, 0:PAD] = slab_edge
        ref[:, PAD + COLS : 2 * PAD + COLS] = slab_edge

    def place_tile(j, p, i):
        sib_copy(j).wait_recv()
        high, low = split(mown[j])
        mh[0:ROWS, :] = high
        ml[0:ROWS, :] = low
        high, low = split(msib[j])
        mh[ROWS : 2 * ROWS, :] = high
        ml[ROWS : 2 * ROWS, :] = low
        xr = XROWS[p]

        def body(k, _):
            dx = (2 - k) & (NX - 1)
            rows = phi[pl.ds(pl.multiple_of(dx * GROUP, GROUP), GROUP), :]
            part = (dot(rows, mh[...]) + dot(rows, ml[...])).reshape(NZ, PATCH, TILE)
            px[p][i, dx] = part[:, :xr]
            pz[p][i, dx] = part[:, xr:]
            return 0

        lax.fori_loop(0, NX, body, 0)

    def message(p, i, m):
        if m < 6:
            dx, first = ((2, 0), (1, 4), (1, 0), (2, 4), (3, 0), (3, 4))[m]
            src, dst = px[p].at[i, dx, pl.ds(first, 4)], xrx[p].at[i, m]
            device = at_x(1 if m < 3 else NX - 1)
        elif m < 14:
            k, cut = m - 6, XCUT[p]
            rows = (
                pl.ds(0, cut) if k == 0
                else pl.ds(cut, XROWS[p] - cut) if k == 4
                else pl.ds(0, XROWS[p])
            )
            src = px[p].at[i, 0, (4, 3, 2, 1, 4, 5, 6, 7)[k], rows]
            dst = xrz[p].at[i, k, rows]
            device = at_z(1 if k < 4 else NZ - 1)
        elif m < 22:
            k = m - 14
            part = pl.ds(0, 2) if k == 0 else pl.ds(2, 2) if k == 4 else pl.ds(0, 4)
            src = pz[p].at[i, part, (4, 3, 2, 1, 4, 5, 6, 7)[k]]
            dst = zrz[p].at[i, k, part]
            device = at_z(1 if k < 4 else NZ - 1)
        else:
            k, cut, zr = m - 22, ZCUT[p], PATCH - XROWS[p]
            low, high = pl.ds(0, cut), pl.ds(cut, zr - cut)
            dx, rows = ((2, low), (1, high), (1, low), (2, high), (3, low), (3, high))[k]
            src, dst = pz[p].at[i, dx, 0, rows], zrx[p].at[i, k, rows]
            device = at_x(1 if k < 3 else NX - 1)
        return remote(src, dst, ssem[p].at[i, m], rsem[p].at[i, m], device)

    def send(p, i, *which):
        for m in which:
            message(p, i, m).start()

    def arrived(p, i, *which):
        for m in which:
            message(p, i, m).wait_recv()

    def stage(age, p, i, j):
        X, Z, A, B, C, D = px[p], pz[p], xrx[p], xrz[p], zrz[p], zrx[p]
        xr, xc, zc = XROWS[p], XCUT[p], ZCUT[p]
        zr = PATCH - xr
        if age == 0:
            send(p, i, 0, 3, 14, 18, 1, 4)
        elif age == 1:
            arrived(p, i, 14)
            Z[i, 0:2, 3] += C[i, 0, 0:2]
            send(p, i, 15)
            arrived(p, i, 18)
            Z[i, 2:4, 5] += C[i, 4, 2:4]
            send(p, i, 19)
            arrived(p, i, 0)
            X[i, 1, 0:4] += A[i, 0]
            send(p, i, 2)
            arrived(p, i, 3)
            X[i, 3, 4:8] += A[i, 3]
            send(p, i, 5)
        elif age == 2:
            arrived(p, i, 15)
            Z[i, :, 2] += C[i, 1]
            send(p, i, 16)
            arrived(p, i, 19)
            Z[i, :, 6] += C[i, 5]
            send(p, i, 20)
            arrived(p, i, 1, 5)
            X[i, 0, 4:8] += A[i, 1] + A[i, 5]
            send(p, i, 6, 10)
            arrived(p, i, 2, 4)
            X[i, 0, 0:4] += A[i, 2] + A[i, 4]
        elif age == 3:
            arrived(p, i, 16)
            Z[i, :, 1] += C[i, 2]
            send(p, i, 17)
            arrived(p, i, 20)
            Z[i, :, 7] += C[i, 6]
            send(p, i, 21)
            arrived(p, i, 6)
            X[i, 0, 3, 0:xc] += B[i, 0, 0:xc]
            send(p, i, 7)
            arrived(p, i, 10)
            X[i, 0, 5, xc:xr] += B[i, 4, xc:xr]
            send(p, i, 11)
        elif age == 4:
            arrived(p, i, 17, 21)
            Z[i, :, 0] += C[i, 3] + C[i, 7]
            send(p, i, 22, 25, 23, 26)
            arrived(p, i, 7)
            X[i, 0, 2] += B[i, 1]
            send(p, i, 8)
            arrived(p, i, 11)
            X[i, 0, 6] += B[i, 5]
            send(p, i, 12)
        elif age == 5:
            arrived(p, i, 22)
            Z[i, 1, 0, 0:zc] += D[i, 0, 0:zc]
            send(p, i, 24)
            arrived(p, i, 25)
            Z[i, 3, 0, zc:zr] += D[i, 3, zc:zr]
            send(p, i, 27)
            arrived(p, i, 8)
            X[i, 0, 1] += B[i, 2]
            send(p, i, 9)
            arrived(p, i, 12)
            X[i, 0, 7] += B[i, 6]
            send(p, i, 13)
        elif age == 6:
            arrived(p, i, 23, 24, 26, 27)
            arrived(p, i, 9, 13)
            parts = [
                X[i, 0, 0] + B[i, 3] + B[i, 7],
                Z[i, 0, 0, 0:zc] + D[i, 2, 0:zc] + D[i, 4, 0:zc],
                Z[i, 0, 0, zc:zr] + D[i, 1, zc:zr] + D[i, 5, zc:zr],
            ]
            scale = inv[...]
            coadd = jnp.concatenate(parts, axis=0) * jnp.concatenate([scale, scale], axis=1)
            coadd_ref[0, :, pl.ds(pl.multiple_of(j * TILE, TILE), TILE)] = coadd
            high, low = split(coadd)
            high, low = split(dot3(tdh[...], tdl[...], high, low))
            start = pl.multiple_of(PAD + j * TILE, 128)
            rch[:, pl.ds(start, TILE)] = high
            rcl[:, pl.ds(start, TILE)] = low
        elif age == 7:
            window = pl.ds(pl.multiple_of(j * TILE, TILE), 2 * TILE)
            smooth = dot3(rch[:, window], rcl[:, window], dch[...], dcl[...])
            sm[j] = smooth.reshape(NB, 16, TILE)
            for d in range(1, NB):
                y_copy(j, d).start()
        else:
            for d in range(1, NB):
                y_copy(j, d).wait_recv()
            total = sm[j, 0] + yr[j, 0] + yr[j, 1] + yr[j, 2]
            det_ref[:, pl.ds(pl.multiple_of(j * TILE, TILE), TILE)] = total[0:SLAB]

    def y_copy(j, d):
        return remote(sm.at[j, d], yr.at[j, d - 1], y_s.at[j, d - 1], y_r.at[j, d - 1], at_y(d))

    def wx_copy(d):
        return remote(wb.at[d], wrx.at[d - 1], w_s.at[d - 1], w_r.at[d - 1], at_x(d))

    def wz_copy(d):
        return remote(wz.at[d], wrz.at[d - 1], w_s.at[d + 2], w_r.at[d + 2], at_z(d))

    diagonal = lax.broadcasted_iota(jnp.int32, (PATCH, 128), 0) == lax.broadcasted_iota(
        jnp.int32, (PATCH, 128), 1
    )

    def weights_out():
        ones = jnp.ones((2 * ROWS, 128), BF16)

        def body(k, _):
            rows = phi[pl.ds(pl.multiple_of(k * GROUP, GROUP), GROUP), :]
            sums = dot(rows, ones).reshape(NZ, PATCH, 128)
            flat = jnp.sum(jnp.where(diagonal[None], sums, 0.0), axis=1, keepdims=True)
            wb[k] = jnp.broadcast_to(flat, (NZ, 8, 128))
            return 0

        lax.fori_loop(0, NX, body, 0)
        for d in range(1, NX):
            wx_copy(d).start()

    def weights_on():
        for d in range(1, NX):
            wx_copy(d).wait_recv()
        wz[...] = wb[0] + wrx[0] + wrx[1] + wrx[2]
        for d in range(1, NZ):
            wz_copy(d).start()

    def weights_in():
        for d in range(1, NZ):
            wz_copy(d).wait_recv()
        total = wz[0]
        for d in range(1, NZ):
            total = total + wrz[d - 1]
        column = jnp.sum(jnp.where(diagonal, total[0:1], 0.0), axis=1, keepdims=True)
        inv[...] = jnp.broadcast_to(1.0 / (1.0 + column), (PATCH, 128))

    def slots(u, _):
        for par in range(2):
            t = 2 * u + par

            @pl.when(t + 2 < NT)
            def _():
                convert(t + 2)

            @pl.when(t + 1 < NT)
            def _():
                correlate(t + 1)

            @pl.when(t < NT)
            def _():
                place_tile(t, par, u)
                stage(0, par, u, t)

            if par == 0:
                pl.when(u == 0)(weights_out)
                pl.when(u == 1)(weights_on)
                pl.when(u == 2)(weights_in)
            for age in range(1, LAST_AGE + 1):
                p = (par - age) % 2
                i = u + (par - age - p) // 2
                j = t - age

                @pl.when((j >= 0) & (j < NT))
                def _():
                    stage(age, p, i, j)

        return 0

    lax.fori_loop(0, (NT + LAST_AGE) // 2, slots, 0)

    def finish(i, _):
        for p in range(2):
            for m in range(28):
                message(p, i, m).wait_send()
            sib_copy(2 * i + p).wait_send()
            for d in range(1, NB):
                y_copy(2 * i + p, d).wait_send()
        return 0

    lax.fori_loop(0, NP, finish, 0)
    meta_copy.wait_send()
    for d in range(1, NX):
        wx_copy(d).wait_send()
    for d in range(1, NZ):
        wz_copy(d).wait_send()


def on_device(images, row_kernel, col_kernel, patch_ids, row_offsets, weight_codes, drt, dct, bw):
    vmem = pl.BlockSpec(memory_space=pltpu.VMEM)
    smem = pl.BlockSpec(memory_space=pltpu.SMEM)
    zrows = tuple(PATCH - r for r in XROWS)
    scratch = [
        pltpu.VMEM((NT, ROWS, TILE), F32),
        pltpu.VMEM((ROWS, COLS + 2 * PAD), BF16),
        pltpu.VMEM((ROWS, COLS + 2 * PAD), BF16),
        pltpu.VMEM((ROWS, ROWS), BF16),
        pltpu.VMEM((ROWS, ROWS), BF16),
        pltpu.VMEM((2 * TILE, TILE), BF16),
        pltpu.VMEM((2 * TILE, TILE), BF16),
        pltpu.VMEM((2 * TILE, TILE), BF16),
        pltpu.VMEM((2 * TILE, TILE), BF16),
        pltpu.VMEM((64, PATCH), BF16),
        pltpu.VMEM((64, PATCH), BF16),
        pltpu.VMEM((8, ROWS), jnp.int32),
        pltpu.VMEM((8, ROWS), jnp.int32),
        pltpu.VMEM((OWN, 2 * ROWS), BF16),
        pltpu.VMEM((NT, ROWS, TILE), F32),
        pltpu.VMEM((NT, ROWS, TILE), F32),
        pltpu.VMEM((2 * ROWS, TILE), BF16),
        pltpu.VMEM((2 * ROWS, TILE), BF16),
    ]
    scratch += [pltpu.VMEM((NP, NX, NZ, r, TILE), F32) for r in XROWS]
    scratch += [pltpu.VMEM((NP, NX, NZ, r, TILE), F32) for r in zrows]
    scratch += [pltpu.VMEM((NP, 6, 4, r, TILE), F32) for r in XROWS]
    scratch += [pltpu.VMEM((NP, 8, r, TILE), F32) for r in XROWS]
    scratch += [pltpu.VMEM((NP, 8, NX, r, TILE), F32) for r in zrows]
    scratch += [pltpu.VMEM((NP, 6, r, TILE), F32) for r in zrows]
    scratch += [
        pltpu.VMEM((NX, NZ, 8, 128), F32),
        pltpu.VMEM((NX - 1, NZ, 8, 128), F32),
        pltpu.VMEM((NZ, 8, 128), F32),
        pltpu.VMEM((NZ - 1, 8, 128), F32),
        pltpu.VMEM((PATCH, 128), F32),
        pltpu.VMEM((64, COLS + 2 * PAD), BF16),
        pltpu.VMEM((64, COLS + 2 * PAD), BF16),
        pltpu.VMEM((NT, NB, 16, TILE), F32),
        pltpu.VMEM((NT, NB - 1, 16, TILE), F32),
    ]
    dma = pltpu.SemaphoreType.DMA
    scratch += [
        dma((NT,)), dma((2,)), dma((NT,)), dma((NT,)),
        dma((NP, 28)), dma((NP, 28)), dma((NP, 28)), dma((NP, 28)),
        dma((NX - 1 + NZ - 1,)), dma((NX - 1 + NZ - 1,)),
        dma((NT, NB - 1)), dma((NT, NB - 1)),
    ]
    return pl.pallas_call(
        kernel,
        out_shape=(
            jax.ShapeDtypeStruct((1, PATCH, COLS), F32),
            jax.ShapeDtypeStruct((SLAB, COLS), F32),
        ),
        in_specs=[pl.BlockSpec(memory_space=pl.ANY), smem, smem, vmem, vmem, vmem, smem, smem, smem],
        out_specs=(vmem, vmem),
        scratch_shapes=scratch,
        compiler_params=pltpu.CompilerParams(
            collective_id=0, has_side_effects=True, vmem_limit_bytes=60 << 20
        ),
        cost_estimate=pl.CostEstimate(
            flops=20_000_000_000, bytes_accessed=5_000_000, transcendentals=0
        ),
    )(images, row_kernel, col_kernel, patch_ids, row_offsets, weight_codes, drt, dct, bw)


def solution(mesh):
    placed = (P("band", "visit", None),) * 6 + (P(), P(), P())
    return jax.shard_map(
        on_device,
        mesh=mesh,
        in_specs=placed,
        out_specs=(P("band", "visit", None), P(("visit", "band"), None)),
        check_vma=False,
    )
```

```python
import jax
import jax.numpy as jnp
from jax import lax
from jax.experimental import pallas as pl
from jax.experimental.pallas import tpu as pltpu
from jax.sharding import PartitionSpec as P

MESH = pl.DeviceIdType.MESH
F32, BF16 = jnp.float32, jnp.bfloat16

COLS = 2048
BLOCK_ROWS = 16
BLOCKS = 32
PATCH = 48
TAPS = 31
HALF = 15
DTAPS = 9
DHALF = 4
ROWS = 512
NX, NZ, NB = 4, 8, 4
TILE = 256
NT = COLS // TILE
PAD = 128
GROUP = NZ * PATCH
OWN = NX * GROUP
FIRST = (0, 2, 4, 8)
XROWS = (16, 24, 32)
XCUT = (8, 16, 16)
ZCUT = (16, 16, 8)
CLASSES = range(len(XROWS))
COUNT = tuple(FIRST[p + 1] - FIRST[p] for p in CLASSES)
SLAB = 12
LAST_AGE = 8
MESSAGES = 30


def split(value):
    high = value.astype(BF16)
    return high, (value - high.astype(F32)).astype(BF16)


def dot(a, b):
    return jnp.dot(a, b, preferred_element_type=F32)


def dot3(a_high, a_low, b_high, b_low):
    return dot(a_high, b_high) + dot(a_low, b_high) + dot(a_high, b_low)


def band_block(taps, shift):
    diff = (
        lax.broadcasted_iota(jnp.int32, (128, 128), 0)
        - lax.broadcasted_iota(jnp.int32, (128, 128), 1)
        + shift
    )
    block = jnp.zeros((128, 128), F32)
    for index, tap in enumerate(taps):
        block = jnp.where(diff == index, tap, block)
    return block


def kernel(
    img, rk_in, ck_in, pid_in, off_in, code_in, drt_in, dct_in, bw_in,
    coadd_out, det_out,
    rk, ck, drt, dct, bw, pid, off, code, coadd, det,
    ximg, xh, xl, trh, trl, tch, tcl, tdh, tdl,
    meta, meta_sib, phi, mown, msib, mh, ml,
    px, pz, xrx, xrz, zrz, zrx,
    wb, wrx, wz, wrz, inv, rc, sm, yr,
    in_sem, out_sem, img_sem, meta_sem, sib_s, sib_r, ssem, rsem, w_s, w_r, y_s, y_r,
):

    v = lax.axis_index("visit")
    b = lax.axis_index("band")
    c = v % 2
    x = (v // 2) % NX
    z = v // (2 * NX)

    def at_x(step):
        return (z * (2 * NX) + ((x + step) % NX) * 2 + c, b)

    def at_z(step):
        return (((z + step) % NZ) * (2 * NX) + x * 2 + c, b)

    def at_y(step):
        return (v, (b + step) % NB)

    sibling = (v + 1 - 2 * c, b)

    def remote(src, dst, send, recv, device):
        return pltpu.make_async_remote_copy(
            src_ref=src, dst_ref=dst, send_sem=send, recv_sem=recv,
            device_id=device, device_id_type=MESH,
        )

    def image_copy(k):
        return pltpu.make_async_copy(
            img.at[0, :, pl.ds(pl.multiple_of(k * TILE, TILE), TILE)], ximg.at[k], img_sem.at[k]
        )

    small = [
        pltpu.make_async_copy(src, dst, in_sem.at[k])
        for k, (src, dst) in enumerate(
            (
                (ck_in, ck), (rk_in, rk), (pid_in, pid), (off_in, off), (code_in, code),
                (drt_in, drt), (dct_in, dct), (bw_in, bw),
            )
        )
    ]
    for copy in small:
        copy.start()
    for k in range(NT):
        image_copy(k).start()

    barrier = pltpu.get_barrier_semaphore()
    partners = (
        [sibling]
        + [at_x(d) for d in range(1, NX)]
        + [at_z(d) for d in range(1, NZ)]
        + [at_y(d) for d in range(1, NB)]
    )
    for partner in partners:
        pl.semaphore_signal(barrier, inc=1, device_id=partner, device_id_type=MESH)

    def spread_lists():
        spread = (
            lax.broadcasted_iota(jnp.int32, (BLOCKS, ROWS), 1) // BLOCK_ROWS
            == lax.broadcasted_iota(jnp.int32, (BLOCKS, ROWS), 0)
        ).astype(F32)
        for copy in small[2:5]:
            copy.wait()
        for k, ref in enumerate((pid, off, code)):
            values = jnp.concatenate([ref[0].astype(F32), jnp.zeros((6, BLOCKS), F32)], axis=0)
            wide = dot(values.astype(BF16), spread.astype(BF16))
            meta[2 * k : 2 * k + 2, :] = wide[0:2].astype(jnp.int32)
        meta[6:8, :] = jnp.zeros((2, ROWS), jnp.int32)

    spread_lists()
    small[0].wait()
    small[1].wait()

    row_taps = [rk[0, 0, m] for m in range(TAPS)]
    col_taps = [ck[0, 0, m] for m in range(TAPS)]
    tch[...] = jnp.zeros(tch.shape, BF16)
    tcl[...] = jnp.zeros(tcl.shape, BF16)
    for d in (-1, 0, 1):
        high, low = split(band_block(col_taps, 128 * d + HALF))
        for cb in range(2):
            ub = d + 1 + cb
            tch[128 * ub : 128 * ub + 128, 128 * cb : 128 * cb + 128] = high
            tcl[128 * ub : 128 * ub + 128, 128 * cb : 128 * cb + 128] = low
    trh[...] = jnp.zeros(trh.shape, BF16)
    trl[...] = jnp.zeros(trl.shape, BF16)
    backward = row_taps[::-1]
    for d in (-1, 0, 1):
        high, low = split(band_block(backward, TAPS - 1 - (128 * d + HALF)))
        for ib in range(4):
            if 0 <= ib + d < 4:
                kb = ib + d
                trh[128 * ib : 128 * ib + 128, 128 * kb : 128 * kb + 128] = high
                trl[128 * ib : 128 * ib + 128, 128 * kb : 128 * kb + 128] = low

    edge = jnp.zeros((ROWS, PAD), BF16)
    for ref in (xh, xl):
        ref[:, 0:PAD] = edge
        ref[:, PAD + COLS : 2 * PAD + COLS] = edge

    def convert(k):
        image_copy(k).wait()
        high, low = split(ximg[k])
        start = pl.multiple_of(PAD + k * TILE, 128)
        xh[:, pl.ds(start, TILE)] = high
        xl[:, pl.ds(start, TILE)] = low

    def sib_copy(j):
        return remote(mown.at[j], msib.at[j], sib_s.at[j], sib_r.at[j], sibling)

    def correlate(j):
        start = pl.multiple_of(j * TILE, TILE)
        window = pl.ds(start, 2 * TILE)
        along = dot3(xh[:, window], xl[:, window], tch[...], tcl[...])
        high, low = split(along)
        mown[j] = dot3(trh[...], trl[...], high, low)
        sib_copy(j).start()

    def owners(source, o):
        ids = source[o : o + 1, :]
        dx = (lax.shift_right_logical(ids, 1) - x) & (NX - 1)
        dz = (lax.shift_right_logical(ids, 3) - z) & (NZ - 1)
        return jnp.where((ids & 1) == c, dx * NZ + dz, -1)

    def targets(source):
        place = lax.broadcasted_iota(jnp.int32, (1, ROWS), 1) % BLOCK_ROWS
        result = []
        for o in range(2):
            owner = owners(source, o)
            row = owner * PATCH + source[2 + o : 3 + o, :] + place
            result.append(jnp.where(owner >= 0, row, -1))
        return result, [source[4 + o : 5 + o, :].astype(F32) for o in range(2)]

    def build_phi(source, first):
        rows, weights = targets(source)
        step = 64

        def body(k, _):
            base = pl.multiple_of(k * step, step)
            index = lax.broadcasted_iota(jnp.int32, (step, ROWS), 0) + base
            value = jnp.where(
                rows[0] == index, weights[0], jnp.where(rows[1] == index, weights[1], 0.0)
            )
            phi[pl.ds(base, step), first : first + ROWS] = value.astype(BF16)
            return 0

        lax.fori_loop(0, OWN // step, body, 0)

    pl.semaphore_wait(barrier, len(partners))
    meta_copy = remote(meta, meta_sib, meta_sem.at[0], meta_sem.at[1], sibling)
    meta_copy.start()
    convert(0)
    convert(1)
    correlate(0)
    build_phi(meta, 0)
    meta_copy.wait_recv()
    build_phi(meta_sib, ROWS)
    convert(2)
    correlate(1)

    for copy in small[5:8]:
        copy.wait()
    dcol_taps = [dct[b, m] for m in range(DTAPS)]
    drow_taps = [bw[b] * drt[b, m] for m in range(DTAPS)]
    out_index = lax.broadcasted_iota(jnp.int32, (64, PATCH), 0)
    out_row = SLAB * ((b + out_index // 16) % NB) + out_index % 16
    tap_index = jnp.where(
        out_index % 16 < SLAB,
        lax.broadcasted_iota(jnp.int32, (64, PATCH), 1) - out_row + DHALF,
        -1,
    )
    drow = jnp.zeros((64, PATCH), F32)
    for index, tap in enumerate(drow_taps):
        drow = jnp.where(tap_index == index, tap, drow)
    high, low = split(drow)
    tdh[...] = high
    tdl[...] = low
    slab_edge = jnp.zeros((64, PAD), F32)
    rc[:, 0:PAD] = slab_edge
    rc[:, PAD + COLS : 2 * PAD + COLS] = slab_edge

    def place_tile(j, p, i):
        sib_copy(j).wait_recv()
        high, low = split(mown[j])
        mh[0:ROWS, :] = high
        ml[0:ROWS, :] = low
        high, low = split(msib[j])
        mh[ROWS : 2 * ROWS, :] = high
        ml[ROWS : 2 * ROWS, :] = low
        xr = XROWS[p]

        def body(k, _):
            first = 2 - 2 * k
            rows = phi[pl.ds(pl.multiple_of(first * GROUP, GROUP), 2 * GROUP), :]
            part = (dot(rows, mh[...]) + dot(rows, ml[...])).reshape(2, NZ, PATCH, TILE)
            px[p][i, pl.ds(first, 2)] = part[:, :, :xr]
            pz[p][i, pl.ds(first, 2)] = part[:, :, xr:]

            @pl.when(k == 0)
            def _():
                send(p, i, 0, 3, 4)

            return 0

        lax.fori_loop(0, NX // 2, body, 0)

    def message(p, i, m):
        if m < 6:
            dx, first = ((2, 0), (1, 4), (1, 0), (2, 4), (3, 0), (3, 4))[m]
            src, dst = px[p].at[i, dx, pl.ds(first, 4)], xrx[p].at[i, m]
            device = at_x(1 if m < 3 else NX - 1)
        elif m < 14:
            k, cut = m - 6, XCUT[p]
            rows = (
                pl.ds(0, cut) if k == 0
                else pl.ds(cut, XROWS[p] - cut) if k == 4
                else pl.ds(0, XROWS[p])
            )
            src = px[p].at[i, 0, (4, 3, 2, 1, 4, 5, 6, 7)[k], rows]
            dst = xrz[p].at[i, k, rows]
            device = at_z(1 if k < 4 else NZ - 1)
        elif m < 22:
            k = m - 14
            part = pl.ds(0, 2) if k in (0, 1) else pl.ds(2, 2) if k in (4, 5) else pl.ds(0, 4)
            src = pz[p].at[i, part, (4, 3, 2, 1, 4, 5, 6, 7)[k]]
            dst = zrz[p].at[i, k, part]
            device = at_z(1 if k < 4 else NZ - 1)
        elif m < 24:
            k, part = ((1, pl.ds(2, 2)), (5, pl.ds(0, 2)))[m - 22]
            src, dst = pz[p].at[i, part, (3, 5)[m - 22]], zrz[p].at[i, k, part]
            device = at_z((1, NZ - 1)[m - 22])
        else:
            k, cut, zr = m - 24, ZCUT[p], PATCH - XROWS[p]
            low, high = pl.ds(0, cut), pl.ds(cut, zr - cut)
            dx, rows = ((2, low), (1, high), (1, low), (2, high), (3, low), (3, high))[k]
            src, dst = pz[p].at[i, dx, 0, rows], zrx[p].at[i, k, rows]
            device = at_x(1 if k < 3 else NX - 1)
        return remote(src, dst, ssem[p].at[i, m], rsem[p].at[i, m], device)

    def send(p, i, *which):
        for m in which:
            message(p, i, m).start()

    def arrived(p, i, *which):
        for m in which:
            message(p, i, m).wait_recv()

    def stage(age, p, i, j):
        X, Z, A, B, C, D = px[p], pz[p], xrx[p], xrz[p], zrz[p], zrx[p]
        xr, xc, zc = XROWS[p], XCUT[p], ZCUT[p]
        zr = PATCH - xr
        if age == 0:
            send(p, i, 14, 18, 22, 23, 1)
        elif age == 1:
            arrived(p, i, 14)
            Z[i, 0:2, 3] += C[i, 0, 0:2]
            send(p, i, 15)
            arrived(p, i, 18)
            Z[i, 2:4, 5] += C[i, 4, 2:4]
            send(p, i, 19)
            arrived(p, i, 0)
            X[i, 1, 0:4] += A[i, 0]
            send(p, i, 2)
            arrived(p, i, 3)
            X[i, 3, 4:8] += A[i, 3]
            send(p, i, 5)
        elif age == 2:
            arrived(p, i, 15, 22)
            Z[i, :, 2] += C[i, 1]
            send(p, i, 16)
            arrived(p, i, 19, 23)
            Z[i, :, 6] += C[i, 5]
            send(p, i, 20)
            arrived(p, i, 1, 5)
            X[i, 0, 4:8] += A[i, 1] + A[i, 5]
            send(p, i, 6, 10)
            arrived(p, i, 2, 4)
            X[i, 0, 0:4] += A[i, 2] + A[i, 4]
        elif age == 3:
            arrived(p, i, 16)
            Z[i, :, 1] += C[i, 2]
            send(p, i, 17)
            arrived(p, i, 20)
            Z[i, :, 7] += C[i, 6]
            send(p, i, 21)
            arrived(p, i, 6)
            X[i, 0, 3, 0:xc] += B[i, 0, 0:xc]
            send(p, i, 7)
            arrived(p, i, 10)
            X[i, 0, 5, xc:xr] += B[i, 4, xc:xr]
            send(p, i, 11)
        elif age == 4:
            arrived(p, i, 17, 21)
            Z[i, :, 0] += C[i, 3] + C[i, 7]
            send(p, i, 24, 27, 25, 28)
            arrived(p, i, 7)
            X[i, 0, 2] += B[i, 1]
            send(p, i, 8)
            arrived(p, i, 11)
            X[i, 0, 6] += B[i, 5]
            send(p, i, 12)
        elif age == 5:
            arrived(p, i, 24)
            Z[i, 1, 0, 0:zc] += D[i, 0, 0:zc]
            send(p, i, 26)
            arrived(p, i, 27)
            Z[i, 3, 0, zc:zr] += D[i, 3, zc:zr]
            send(p, i, 29)
            arrived(p, i, 8)
            X[i, 0, 1] += B[i, 2]
            send(p, i, 9)
            arrived(p, i, 12)
            X[i, 0, 7] += B[i, 6]
            send(p, i, 13)
        elif age == 6:
            arrived(p, i, 25, 26, 28, 29)
            arrived(p, i, 9, 13)
            parts = [
                X[i, 0, 0] + B[i, 3] + B[i, 7],
                Z[i, 0, 0, 0:zc] + D[i, 2, 0:zc] + D[i, 4, 0:zc],
                Z[i, 0, 0, zc:zr] + D[i, 1, zc:zr] + D[i, 5, zc:zr],
            ]
            scale = inv[...]
            value = jnp.concatenate(parts, axis=0) * jnp.concatenate([scale, scale], axis=1)
            coadd[j] = value
            coadd_copy(j).start()
            high, low = split(value)
            start = pl.multiple_of(PAD + j * TILE, 128)
            rc[:, pl.ds(start, TILE)] = dot3(tdh[...], tdl[...], high, low)
        elif age == 7:
            window = rc[:, pl.ds(pl.multiple_of(j * TILE, TILE), 2 * TILE)]
            smooth = dcol_taps[DHALF] * window[:, PAD : PAD + TILE]
            for m in range(DTAPS):
                if m != DHALF:
                    moved = pltpu.roll(window, (DHALF - m) % (2 * TILE), 1)
                    smooth = smooth + dcol_taps[m] * moved[:, PAD : PAD + TILE]
            sm[j] = smooth.reshape(NB, 16, TILE)
            for d in range(1, NB):
                y_copy(j, d).start()
        else:
            for d in range(1, NB):
                y_copy(j, d).wait_recv()
            total = sm[j, 0] + yr[j, 0] + yr[j, 1] + yr[j, 2]
            det[j] = total[0:SLAB]
            det_copy(j).start()
            for m in range(MESSAGES):
                message(p, i, m).wait_send()
            sib_copy(j).wait_send()
            for d in range(1, NB):
                y_copy(j, d).wait_send()
            coadd_copy(j).wait()

    def columns(j):
        return pl.ds(pl.multiple_of(j * TILE, TILE), TILE)

    def coadd_copy(j):
        return pltpu.make_async_copy(coadd.at[j], coadd_out.at[0, :, columns(j)], out_sem.at[0, j])

    def det_copy(j):
        return pltpu.make_async_copy(det.at[j], det_out.at[:, columns(j)], out_sem.at[1, j])

    def y_copy(j, d):
        return remote(sm.at[j, d], yr.at[j, d - 1], y_s.at[j, d - 1], y_r.at[j, d - 1], at_y(d))

    def wx_copy(d):
        return remote(wb.at[d], wrx.at[d - 1], w_s.at[d - 1], w_r.at[d - 1], at_x(d))

    def wz_copy(d):
        return remote(wz.at[d], wrz.at[d - 1], w_s.at[d + 2], w_r.at[d + 2], at_z(d))

    diagonal = lax.broadcasted_iota(jnp.int32, (PATCH, 128), 0) == lax.broadcasted_iota(
        jnp.int32, (PATCH, 128), 1
    )

    def weights_out():
        group = lax.broadcasted_iota(jnp.int32, (NX * NZ, ROWS), 0)
        depth = lax.broadcasted_iota(jnp.int32, (PATCH, ROWS), 0)
        head = lax.broadcasted_iota(jnp.int32, (1, ROWS), 1) % BLOCK_ROWS == 0
        sums = jnp.zeros((NX * NZ, PATCH), F32)
        for source in (meta, meta_sib):
            for o in range(2):
                owner = owners(source, o)
                weight = jnp.where(head, source[4 + o : 5 + o, :].astype(F32), 0.0)
                start = source[2 + o : 3 + o, :]
                left = jnp.where(owner == group, weight, 0.0).astype(BF16)
                right = jnp.where((start <= depth) & (depth < start + BLOCK_ROWS), 1.0, 0.0)
                sums = sums + lax.dot_general(
                    left, right.astype(BF16), (((1,), (1,)), ((), ())), preferred_element_type=F32
                )
        sums = jnp.concatenate([sums, jnp.zeros((NX * NZ, 128 - PATCH), F32)], axis=1)
        wb[...] = jnp.broadcast_to(sums[:, None, :], (NX * NZ, 8, 128)).reshape(NX, NZ, 8, 128)
        for d in range(1, NX):
            wx_copy(d).start()

    def weights_on():
        for d in range(1, NX):
            wx_copy(d).wait_recv()
        wz[...] = wb[0] + wrx[0] + wrx[1] + wrx[2]
        for d in range(1, NZ):
            wz_copy(d).start()

    def weights_in():
        for d in range(1, NZ):
            wz_copy(d).wait_recv()
        total = wz[0]
        for d in range(1, NZ):
            total = total + wrz[d - 1]
        column = jnp.sum(jnp.where(diagonal, total[0:1], 0.0), axis=1, keepdims=True)
        inv[...] = jnp.broadcast_to(1.0 / (1.0 + column), (PATCH, 128))

    def in_class(j, p):
        return (j >= FIRST[p]) & (j < FIRST[p + 1])

    def slots(t, _):
        for p in CLASSES:

            @pl.when(in_class(t, p))
            def _():
                place_tile(t, p, t - FIRST[p])
                stage(0, p, t - FIRST[p], t)

        @pl.when(t + 3 < NT)
        def _():
            convert(t + 3)

        @pl.when(t + 2 < NT)
        def _():
            correlate(t + 2)

        pl.when(t == 0)(weights_out)
        pl.when(t == 2)(weights_on)
        pl.when(t == 6)(weights_in)
        for age in range(1, LAST_AGE + 1):
            j = t - age
            for p in CLASSES:

                @pl.when(in_class(j, p))
                def _():
                    stage(age, p, j - FIRST[p], j)

        return 0

    lax.fori_loop(0, NT + LAST_AGE, slots, 0)

    def finish(j, _):
        det_copy(j).wait()
        return 0

    lax.fori_loop(0, NT, finish, 0)
    meta_copy.wait_send()
    for d in range(1, NX):
        wx_copy(d).wait_send()
    for d in range(1, NZ):
        wz_copy(d).wait_send()


def on_device(images, row_kernel, col_kernel, patch_ids, row_offsets, weight_codes, drt, dct, bw):
    anywhere = pl.BlockSpec(memory_space=pl.ANY)
    lists = [jnp.swapaxes(a, 1, 2) for a in (patch_ids, row_offsets, weight_codes)]
    scratch = [
        pltpu.SMEM((1, 1, TAPS), F32),
        pltpu.SMEM((1, 1, TAPS), F32),
        pltpu.SMEM((NB, DTAPS), F32),
        pltpu.SMEM((NB, DTAPS), F32),
        pltpu.SMEM((NB,), F32),
        pltpu.VMEM((1, 2, BLOCKS), jnp.int32),
        pltpu.VMEM((1, 2, BLOCKS), jnp.int32),
        pltpu.VMEM((1, 2, BLOCKS), jnp.int32),
        pltpu.VMEM((NT, PATCH, TILE), F32),
        pltpu.VMEM((NT, SLAB, TILE), F32),
        pltpu.VMEM((NT, ROWS, TILE), F32),
        pltpu.VMEM((ROWS, COLS + 2 * PAD), BF16),
        pltpu.VMEM((ROWS, COLS + 2 * PAD), BF16),
        pltpu.VMEM((ROWS, ROWS), BF16),
        pltpu.VMEM((ROWS, ROWS), BF16),
        pltpu.VMEM((2 * TILE, TILE), BF16),
        pltpu.VMEM((2 * TILE, TILE), BF16),
        pltpu.VMEM((64, PATCH), BF16),
        pltpu.VMEM((64, PATCH), BF16),
        pltpu.VMEM((8, ROWS), jnp.int32),
        pltpu.VMEM((8, ROWS), jnp.int32),
        pltpu.VMEM((OWN, 2 * ROWS), BF16),
        pltpu.VMEM((NT, ROWS, TILE), F32),
        pltpu.VMEM((NT, ROWS, TILE), F32),
        pltpu.VMEM((2 * ROWS, TILE), BF16),
        pltpu.VMEM((2 * ROWS, TILE), BF16),
    ]
    def per_class(shape):
        return [shape(COUNT[p], XROWS[p], PATCH - XROWS[p]) for p in CLASSES]

    scratch += [
        per_class(lambda n, xr, zr: pltpu.VMEM((n, NX, NZ, xr, TILE), F32)),
        per_class(lambda n, xr, zr: pltpu.VMEM((n, NX, NZ, zr, TILE), F32)),
        per_class(lambda n, xr, zr: pltpu.VMEM((n, 6, 4, xr, TILE), F32)),
        per_class(lambda n, xr, zr: pltpu.VMEM((n, 8, xr, TILE), F32)),
        per_class(lambda n, xr, zr: pltpu.VMEM((n, 8, NX, zr, TILE), F32)),
        per_class(lambda n, xr, zr: pltpu.VMEM((n, 6, zr, TILE), F32)),
    ]
    scratch += [
        pltpu.VMEM((NX, NZ, 8, 128), F32),
        pltpu.VMEM((NX - 1, NZ, 8, 128), F32),
        pltpu.VMEM((NZ, 8, 128), F32),
        pltpu.VMEM((NZ - 1, 8, 128), F32),
        pltpu.VMEM((PATCH, 128), F32),
        pltpu.VMEM((64, COLS + 2 * PAD), F32),
        pltpu.VMEM((NT, NB, 16, TILE), F32),
        pltpu.VMEM((NT, NB - 1, 16, TILE), F32),
    ]
    dma = pltpu.SemaphoreType.DMA
    scratch += [
        dma((8,)), dma((2, NT)), dma((NT,)), dma((2,)), dma((NT,)), dma((NT,)),
        per_class(lambda n, xr, zr: dma((n, MESSAGES))),
        per_class(lambda n, xr, zr: dma((n, MESSAGES))),
        dma((NX - 1 + NZ - 1,)), dma((NX - 1 + NZ - 1,)),
        dma((NT, NB - 1)), dma((NT, NB - 1)),
    ]
    return pl.pallas_call(
        kernel,
        out_shape=(
            jax.ShapeDtypeStruct((1, PATCH, COLS), F32),
            jax.ShapeDtypeStruct((SLAB, COLS), F32),
        ),
        in_specs=[anywhere] * 9,
        out_specs=(anywhere, anywhere),
        scratch_shapes=scratch,
        compiler_params=pltpu.CompilerParams(
            collective_id=0, has_side_effects=True, vmem_limit_bytes=60 << 20
        ),
        cost_estimate=pl.CostEstimate(
            flops=20_000_000_000, bytes_accessed=5_000_000, transcendentals=0
        ),
    )(images, row_kernel, col_kernel, *lists, drt, dct, bw)


def solution(mesh):
    placed = (P("band", "visit", None),) * 6 + (P(), P(), P())
    return jax.shard_map(
        on_device,
        mesh=mesh,
        in_specs=placed,
        out_specs=(P("band", "visit", None), P(("visit", "band"), None)),
        check_vma=False,
    )
```

```python
import jax
import jax.numpy as jnp
from jax import lax
from jax.experimental import pallas as pl
from jax.experimental.pallas import tpu as pltpu
from jax.sharding import PartitionSpec as P

MESH = pl.DeviceIdType.MESH
F32, BF16 = jnp.float32, jnp.bfloat16

COLS = 2048
BLOCK_ROWS = 16
BLOCKS = 32
PATCH = 48
TAPS = 31
HALF = 15
DTAPS = 9
DHALF = 4
ROWS = 512
NX, NZ, NB = 4, 8, 4
TILE = 256
NT = COLS // TILE
PAD = 128
GROUP = NZ * PATCH
OWN = NX * GROUP
FIRST = (0, 2, 4, 8)
XROWS = (16, 24, 32)
XCUT = (8, 16, 16)
ZCUT = (16, 16, 8)
CLASSES = range(len(XROWS))
COUNT = tuple(FIRST[p + 1] - FIRST[p] for p in CLASSES)
SLAB = 12
LAST_AGE = 8
MESSAGES = 30


def split(value):
    high = value.astype(BF16)
    return high, (value - high.astype(F32)).astype(BF16)


def dot(a, b):
    return jnp.dot(a, b, preferred_element_type=F32)


def dot3(a_high, a_low, b_high, b_low):
    return dot(a_high, b_high) + dot(a_low, b_high) + dot(a_high, b_low)


def band_block(taps, shift):
    diff = (
        lax.broadcasted_iota(jnp.int32, (128, 128), 0)
        - lax.broadcasted_iota(jnp.int32, (128, 128), 1)
        + shift
    )
    block = jnp.zeros((128, 128), F32)
    for index, tap in enumerate(taps):
        block = jnp.where(diff == index, tap, block)
    return block


def kernel(
    img, rk_in, ck_in, pid_in, off_in, code_in, drt_in, dct_in, bw_in,
    coadd_out, det_out,
    rk, ck, drt, dct, bw, pid, off, code, coadd, det,
    ximg, xh, xl, trh, trl, tch, tcl, tdh, tdl,
    meta, meta_sib, phi, mown, msib, mh, ml,
    px, pz, xrx, xrz, zrz, zrx,
    wb, wrx, wz, wrz, inv, rc, sm, yr,
    in_sem, out_sem, img_sem, meta_sem, sib_s, sib_r, ssem, rsem, w_s, w_r, y_s, y_r,
):

    v = lax.axis_index("visit")
    b = lax.axis_index("band")
    c = v % 2
    x = (v // 2) % NX
    z = v // (2 * NX)

    def at_x(step):
        return (z * (2 * NX) + ((x + step) % NX) * 2 + c, b)

    def at_z(step):
        return (((z + step) % NZ) * (2 * NX) + x * 2 + c, b)

    def at_y(step):
        return (v, (b + step) % NB)

    sibling = (v + 1 - 2 * c, b)

    def remote(src, dst, send, recv, device):
        return pltpu.make_async_remote_copy(
            src_ref=src, dst_ref=dst, send_sem=send, recv_sem=recv,
            device_id=device, device_id_type=MESH,
        )

    def image_copy(k):
        return pltpu.make_async_copy(
            img.at[0, :, pl.ds(pl.multiple_of(k * TILE, TILE), TILE)], ximg.at[k], img_sem.at[k]
        )

    small = [
        pltpu.make_async_copy(src, dst, in_sem.at[k])
        for k, (src, dst) in enumerate(
            (
                (ck_in, ck), (rk_in, rk), (pid_in, pid), (off_in, off), (code_in, code),
                (drt_in, drt), (dct_in, dct), (bw_in, bw),
            )
        )
    ]
    for copy in small:
        copy.start()
    for k in range(NT):
        image_copy(k).start()

    barrier = pltpu.get_barrier_semaphore()
    partners = (
        [sibling]
        + [at_x(d) for d in range(1, NX)]
        + [at_z(d) for d in range(1, NZ)]
        + [at_y(d) for d in range(1, NB)]
    )
    for partner in partners:
        pl.semaphore_signal(barrier, inc=1, device_id=partner, device_id_type=MESH)

    def spread_lists():
        spread = (
            lax.broadcasted_iota(jnp.int32, (BLOCKS, ROWS), 1) // BLOCK_ROWS
            == lax.broadcasted_iota(jnp.int32, (BLOCKS, ROWS), 0)
        ).astype(F32)
        for copy in small[2:5]:
            copy.wait()
        for k, ref in enumerate((pid, off, code)):
            values = jnp.concatenate([ref[0].astype(F32), jnp.zeros((6, BLOCKS), F32)], axis=0)
            wide = dot(values.astype(BF16), spread.astype(BF16))
            meta[2 * k : 2 * k + 2, :] = wide[0:2].astype(jnp.int32)
        meta[6:8, :] = jnp.zeros((2, ROWS), jnp.int32)

    spread_lists()
    small[0].wait()
    small[1].wait()

    row_taps = [rk[0, 0, m] for m in range(TAPS)]
    col_taps = [ck[0, 0, m] for m in range(TAPS)]
    tch[...] = jnp.zeros(tch.shape, BF16)
    tcl[...] = jnp.zeros(tcl.shape, BF16)
    for d in (-1, 0, 1):
        high, low = split(band_block(col_taps, 128 * d + HALF))
        for cb in range(2):
            ub = d + 1 + cb
            tch[128 * ub : 128 * ub + 128, 128 * cb : 128 * cb + 128] = high
            tcl[128 * ub : 128 * ub + 128, 128 * cb : 128 * cb + 128] = low
    trh[...] = jnp.zeros(trh.shape, BF16)
    trl[...] = jnp.zeros(trl.shape, BF16)
    backward = row_taps[::-1]
    for d in (-1, 0, 1):
        high, low = split(band_block(backward, TAPS - 1 - (128 * d + HALF)))
        for ib in range(4):
            if 0 <= ib + d < 4:
                kb = ib + d
                trh[128 * ib : 128 * ib + 128, 128 * kb : 128 * kb + 128] = high
                trl[128 * ib : 128 * ib + 128, 128 * kb : 128 * kb + 128] = low

    edge = jnp.zeros((ROWS, PAD), BF16)
    for ref in (xh, xl):
        ref[:, 0:PAD] = edge
        ref[:, PAD + COLS : 2 * PAD + COLS] = edge

    def convert(k):
        image_copy(k).wait()
        high, low = split(ximg[k])
        start = pl.multiple_of(PAD + k * TILE, 128)
        xh[:, pl.ds(start, TILE)] = high
        xl[:, pl.ds(start, TILE)] = low

    def sib_copy(j):
        return remote(mown.at[j], msib.at[j], sib_s.at[j], sib_r.at[j], sibling)

    def correlate(j):
        start = pl.multiple_of(j * TILE, TILE)
        window = pl.ds(start, 2 * TILE)
        along = dot3(xh[:, window], xl[:, window], tch[...], tcl[...])
        high, low = split(along)
        mown[j] = dot3(trh[...], trl[...], high, low)
        sib_copy(j).start()

    def owners(source, o):
        ids = source[o : o + 1, :]
        dx = (lax.shift_right_logical(ids, 1) - x) & (NX - 1)
        dz = (lax.shift_right_logical(ids, 3) - z) & (NZ - 1)
        return jnp.where((ids & 1) == c, dx * NZ + dz, -1)

    def targets(source):
        place = lax.broadcasted_iota(jnp.int32, (1, ROWS), 1) % BLOCK_ROWS
        result = []
        for o in range(2):
            owner = owners(source, o)
            row = owner * PATCH + source[2 + o : 3 + o, :] + place
            result.append(jnp.where(owner >= 0, row, -1))
        return result, [source[4 + o : 5 + o, :].astype(F32) for o in range(2)]

    def build_phi(source, first):
        rows, weights = targets(source)
        step = 64

        def body(k, _):
            base = pl.multiple_of(k * step, step)
            index = lax.broadcasted_iota(jnp.int32, (step, ROWS), 0) + base
            value = jnp.where(
                rows[0] == index, weights[0], jnp.where(rows[1] == index, weights[1], 0.0)
            )
            phi[pl.ds(base, step), first : first + ROWS] = value.astype(BF16)
            return 0

        lax.fori_loop(0, OWN // step, body, 0)

    pl.semaphore_wait(barrier, len(partners))
    meta_copy = remote(meta, meta_sib, meta_sem.at[0], meta_sem.at[1], sibling)
    meta_copy.start()
    convert(0)
    convert(1)
    correlate(0)
    build_phi(meta, 0)
    meta_copy.wait_recv()
    build_phi(meta_sib, ROWS)
    convert(2)
    correlate(1)

    for copy in small[5:8]:
        copy.wait()
    dcol_taps = [dct[b, m] for m in range(DTAPS)]
    drow_taps = [bw[b] * drt[b, m] for m in range(DTAPS)]
    out_index = lax.broadcasted_iota(jnp.int32, (64, PATCH), 0)
    out_row = SLAB * ((b + out_index // 16) % NB) + out_index % 16
    tap_index = jnp.where(
        out_index % 16 < SLAB,
        lax.broadcasted_iota(jnp.int32, (64, PATCH), 1) - out_row + DHALF,
        -1,
    )
    drow = jnp.zeros((64, PATCH), F32)
    for index, tap in enumerate(drow_taps):
        drow = jnp.where(tap_index == index, tap, drow)
    high, low = split(drow)
    tdh[...] = high
    tdl[...] = low
    slab_edge = jnp.zeros((64, PAD), F32)
    rc[:, 0:PAD] = slab_edge
    rc[:, PAD + COLS : 2 * PAD + COLS] = slab_edge

    def place_tile(j, p, i):
        sib_copy(j).wait_recv()
        high, low = split(mown[j])
        mh[0:ROWS, :] = high
        ml[0:ROWS, :] = low
        high, low = split(msib[j])
        mh[ROWS : 2 * ROWS, :] = high
        ml[ROWS : 2 * ROWS, :] = low
        xr = XROWS[p]

        def body(k, _):
            first = 2 - 2 * k
            rows = phi[pl.ds(pl.multiple_of(first * GROUP, GROUP), 2 * GROUP), :]
            part = (dot(rows, mh[...]) + dot(rows, ml[...])).reshape(2, NZ, PATCH, TILE)
            px[p][i, pl.ds(first, 2)] = part[:, :, :xr]
            pz[p][i, pl.ds(first, 2)] = part[:, :, xr:]

            @pl.when(k == 0)
            def _():
                send(p, i, 0, 3, 4)

            return 0

        lax.fori_loop(0, NX // 2, body, 0)

    def message(p, i, m):
        if m < 6:
            dx, first = ((2, 0), (1, 4), (1, 0), (2, 4), (3, 0), (3, 4))[m]
            src, dst = px[p].at[i, dx, pl.ds(first, 4)], xrx[p].at[i, m]
            device = at_x(1 if m < 3 else NX - 1)
        elif m < 14:
            k, cut = m - 6, XCUT[p]
            rows = (
                pl.ds(0, cut) if k == 0
                else pl.ds(cut, XROWS[p] - cut) if k == 4
                else pl.ds(0, XROWS[p])
            )
            src = px[p].at[i, 0, (4, 3, 2, 1, 4, 5, 6, 7)[k], rows]
            dst = xrz[p].at[i, k, rows]
            device = at_z(1 if k < 4 else NZ - 1)
        elif m < 22:
            k = m - 14
            part = pl.ds(0, 2) if k in (0, 1) else pl.ds(2, 2) if k in (4, 5) else pl.ds(0, 4)
            src = pz[p].at[i, part, (4, 3, 2, 1, 4, 5, 6, 7)[k]]
            dst = zrz[p].at[i, k, part]
            device = at_z(1 if k < 4 else NZ - 1)
        elif m < 24:
            k, part = ((1, pl.ds(2, 2)), (5, pl.ds(0, 2)))[m - 22]
            src, dst = pz[p].at[i, part, (3, 5)[m - 22]], zrz[p].at[i, k, part]
            device = at_z((1, NZ - 1)[m - 22])
        else:
            k, cut, zr = m - 24, ZCUT[p], PATCH - XROWS[p]
            low, high = pl.ds(0, cut), pl.ds(cut, zr - cut)
            dx, rows = ((2, low), (1, high), (1, low), (2, high), (3, low), (3, high))[k]
            src, dst = pz[p].at[i, dx, 0, rows], zrx[p].at[i, k, rows]
            device = at_x(1 if k < 3 else NX - 1)
        return remote(src, dst, ssem[p].at[i, m], rsem[p].at[i, m], device)

    def send(p, i, *which):
        for m in which:
            message(p, i, m).start()

    def arrived(p, i, *which):
        for m in which:
            message(p, i, m).wait_recv()

    def stage(age, p, i, j):
        X, Z, A, B, C, D = px[p], pz[p], xrx[p], xrz[p], zrz[p], zrx[p]
        xr, xc, zc = XROWS[p], XCUT[p], ZCUT[p]
        zr = PATCH - xr
        if age == 0:
            send(p, i, 14, 18, 22, 23, 1)
        elif age == 1:
            arrived(p, i, 14)
            Z[i, 0:2, 3] += C[i, 0, 0:2]
            send(p, i, 15)
            arrived(p, i, 18)
            Z[i, 2:4, 5] += C[i, 4, 2:4]
            send(p, i, 19)
            arrived(p, i, 0)
            X[i, 1, 0:4] += A[i, 0]
            send(p, i, 2)
            arrived(p, i, 3)
            X[i, 3, 4:8] += A[i, 3]
            send(p, i, 5)
        elif age == 2:
            arrived(p, i, 15, 22)
            Z[i, :, 2] += C[i, 1]
            send(p, i, 16)
            arrived(p, i, 19, 23)
            Z[i, :, 6] += C[i, 5]
            send(p, i, 20)
            arrived(p, i, 1, 5)
            X[i, 0, 4:8] += A[i, 1] + A[i, 5]
            send(p, i, 6, 10)
            arrived(p, i, 2, 4)
            X[i, 0, 0:4] += A[i, 2] + A[i, 4]
        elif age == 3:
            arrived(p, i, 16)
            Z[i, :, 1] += C[i, 2]
            send(p, i, 17)
            arrived(p, i, 20)
            Z[i, :, 7] += C[i, 6]
            send(p, i, 21)
            arrived(p, i, 6)
            X[i, 0, 3, 0:xc] += B[i, 0, 0:xc]
            send(p, i, 7)
            arrived(p, i, 10)
            X[i, 0, 5, xc:xr] += B[i, 4, xc:xr]
            send(p, i, 11)
        elif age == 4:
            arrived(p, i, 17, 21)
            Z[i, :, 0] += C[i, 3] + C[i, 7]
            send(p, i, 24, 27, 25, 28)
            arrived(p, i, 7)
            X[i, 0, 2] += B[i, 1]
            send(p, i, 8)
            arrived(p, i, 11)
            X[i, 0, 6] += B[i, 5]
            send(p, i, 12)
        elif age == 5:
            arrived(p, i, 24)
            Z[i, 1, 0, 0:zc] += D[i, 0, 0:zc]
            send(p, i, 26)
            arrived(p, i, 27)
            Z[i, 3, 0, zc:zr] += D[i, 3, zc:zr]
            send(p, i, 29)
            arrived(p, i, 8)
            X[i, 0, 1] += B[i, 2]
            send(p, i, 9)
            arrived(p, i, 12)
            X[i, 0, 7] += B[i, 6]
            send(p, i, 13)
        elif age == 6:
            arrived(p, i, 25, 26, 28, 29)
            arrived(p, i, 9, 13)
            parts = [
                X[i, 0, 0] + B[i, 3] + B[i, 7],
                Z[i, 0, 0, 0:zc] + D[i, 2, 0:zc] + D[i, 4, 0:zc],
                Z[i, 0, 0, zc:zr] + D[i, 1, zc:zr] + D[i, 5, zc:zr],
            ]
            scale = inv[...]
            value = jnp.concatenate(parts, axis=0) * jnp.concatenate([scale, scale], axis=1)
            coadd[j] = value
            coadd_copy(j).start()
            high, low = split(value)
            start = pl.multiple_of(PAD + j * TILE, 128)
            rc[:, pl.ds(start, TILE)] = dot3(tdh[...], tdl[...], high, low)
        elif age == 7:
            window = rc[:, pl.ds(pl.multiple_of(j * TILE, TILE), 2 * TILE)]
            smooth = dcol_taps[DHALF] * window[:, PAD : PAD + TILE]
            for m in range(DTAPS):
                if m != DHALF:
                    moved = pltpu.roll(window, (DHALF - m) % (2 * TILE), 1)
                    smooth = smooth + dcol_taps[m] * moved[:, PAD : PAD + TILE]
            sm[j] = smooth.reshape(NB, 16, TILE)
            for d in range(1, NB):
                y_copy(j, d).start()
        else:
            for d in range(1, NB):
                y_copy(j, d).wait_recv()
            total = sm[j, 0] + yr[j, 0] + yr[j, 1] + yr[j, 2]
            det[j] = total[0:SLAB]
            det_copy(j).start()
            for m in range(MESSAGES):
                message(p, i, m).wait_send()
            sib_copy(j).wait_send()
            for d in range(1, NB):
                y_copy(j, d).wait_send()
            coadd_copy(j).wait()

    def columns(j):
        return pl.ds(pl.multiple_of(j * TILE, TILE), TILE)

    def coadd_copy(j):
        return pltpu.make_async_copy(coadd.at[j], coadd_out.at[0, :, columns(j)], out_sem.at[0, j])

    def det_copy(j):
        return pltpu.make_async_copy(det.at[j], det_out.at[:, columns(j)], out_sem.at[1, j])

    def y_copy(j, d):
        return remote(sm.at[j, d], yr.at[j, d - 1], y_s.at[j, d - 1], y_r.at[j, d - 1], at_y(d))

    def wx_copy(d):
        return remote(wb.at[d], wrx.at[d - 1], w_s.at[d - 1], w_r.at[d - 1], at_x(d))

    def wz_copy(d):
        return remote(wz.at[d], wrz.at[d - 1], w_s.at[d + 2], w_r.at[d + 2], at_z(d))

    diagonal = lax.broadcasted_iota(jnp.int32, (PATCH, 128), 0) == lax.broadcasted_iota(
        jnp.int32, (PATCH, 128), 1
    )

    def weights_out():
        group = lax.broadcasted_iota(jnp.int32, (NX * NZ, ROWS), 0)
        depth = lax.broadcasted_iota(jnp.int32, (PATCH, ROWS), 0)
        head = lax.broadcasted_iota(jnp.int32, (1, ROWS), 1) % BLOCK_ROWS == 0
        sums = jnp.zeros((NX * NZ, PATCH), F32)
        for source in (meta, meta_sib):
            for o in range(2):
                owner = owners(source, o)
                weight = jnp.where(head, source[4 + o : 5 + o, :].astype(F32), 0.0)
                start = source[2 + o : 3 + o, :]
                left = jnp.where(owner == group, weight, 0.0).astype(BF16)
                right = jnp.where((start <= depth) & (depth < start + BLOCK_ROWS), 1.0, 0.0)
                sums = sums + lax.dot_general(
                    left, right.astype(BF16), (((1,), (1,)), ((), ())), preferred_element_type=F32
                )
        sums = jnp.concatenate([sums, jnp.zeros((NX * NZ, 128 - PATCH), F32)], axis=1)
        wb[...] = jnp.broadcast_to(sums[:, None, :], (NX * NZ, 8, 128)).reshape(NX, NZ, 8, 128)
        for d in range(1, NX):
            wx_copy(d).start()

    def weights_on():
        for d in range(1, NX):
            wx_copy(d).wait_recv()
        wz[...] = wb[0] + wrx[0] + wrx[1] + wrx[2]
        for d in range(1, NZ):
            wz_copy(d).start()

    def weights_in():
        for d in range(1, NZ):
            wz_copy(d).wait_recv()
        total = wz[0]
        for d in range(1, NZ):
            total = total + wrz[d - 1]
        column = jnp.sum(jnp.where(diagonal, total[0:1], 0.0), axis=1, keepdims=True)
        inv[...] = jnp.broadcast_to(1.0 / (1.0 + column), (PATCH, 128))

    def in_class(j, p):
        return (j >= FIRST[p]) & (j < FIRST[p + 1])

    def slots(t, _):
        for p in CLASSES:

            @pl.when(in_class(t, p))
            def _():
                place_tile(t, p, t - FIRST[p])
                stage(0, p, t - FIRST[p], t)

        @pl.when(t + 3 < NT)
        def _():
            convert(t + 3)

        @pl.when(t + 2 < NT)
        def _():
            correlate(t + 2)

        pl.when(t == 0)(weights_out)
        pl.when(t == 2)(weights_on)
        pl.when(t == 6)(weights_in)
        for age in range(1, LAST_AGE + 1):
            j = t - age
            for p in CLASSES:

                @pl.when(in_class(j, p))
                def _():
                    stage(age, p, j - FIRST[p], j)

        return 0

    lax.fori_loop(0, NT + LAST_AGE, slots, 0)

    def finish(j, _):
        det_copy(j).wait()
        return 0

    lax.fori_loop(0, NT, finish, 0)
    meta_copy.wait_send()
    for d in range(1, NX):
        wx_copy(d).wait_send()
    for d in range(1, NZ):
        wz_copy(d).wait_send()


def hand_over(coadd, detection, coadd_out, detection_out):
    coadd_out[...] = coadd[...]
    detection_out[...] = detection[...]


def on_device(images, row_kernel, col_kernel, patch_ids, row_offsets, weight_codes, drt, dct, bw):
    anywhere = pl.BlockSpec(memory_space=pl.ANY)
    lists = [jnp.swapaxes(a, 1, 2) for a in (patch_ids, row_offsets, weight_codes)]
    scratch = [
        pltpu.SMEM((1, 1, TAPS), F32),
        pltpu.SMEM((1, 1, TAPS), F32),
        pltpu.SMEM((NB, DTAPS), F32),
        pltpu.SMEM((NB, DTAPS), F32),
        pltpu.SMEM((NB,), F32),
        pltpu.VMEM((1, 2, BLOCKS), jnp.int32),
        pltpu.VMEM((1, 2, BLOCKS), jnp.int32),
        pltpu.VMEM((1, 2, BLOCKS), jnp.int32),
        pltpu.VMEM((NT, PATCH, TILE), F32),
        pltpu.VMEM((NT, SLAB, TILE), F32),
        pltpu.VMEM((NT, ROWS, TILE), F32),
        pltpu.VMEM((ROWS, COLS + 2 * PAD), BF16),
        pltpu.VMEM((ROWS, COLS + 2 * PAD), BF16),
        pltpu.VMEM((ROWS, ROWS), BF16),
        pltpu.VMEM((ROWS, ROWS), BF16),
        pltpu.VMEM((2 * TILE, TILE), BF16),
        pltpu.VMEM((2 * TILE, TILE), BF16),
        pltpu.VMEM((64, PATCH), BF16),
        pltpu.VMEM((64, PATCH), BF16),
        pltpu.VMEM((8, ROWS), jnp.int32),
        pltpu.VMEM((8, ROWS), jnp.int32),
        pltpu.VMEM((OWN, 2 * ROWS), BF16),
        pltpu.VMEM((NT, ROWS, TILE), F32),
        pltpu.VMEM((NT, ROWS, TILE), F32),
        pltpu.VMEM((2 * ROWS, TILE), BF16),
        pltpu.VMEM((2 * ROWS, TILE), BF16),
    ]
    def per_class(shape):
        return [shape(COUNT[p], XROWS[p], PATCH - XROWS[p]) for p in CLASSES]

    scratch += [
        per_class(lambda n, xr, zr: pltpu.VMEM((n, NX, NZ, xr, TILE), F32)),
        per_class(lambda n, xr, zr: pltpu.VMEM((n, NX, NZ, zr, TILE), F32)),
        per_class(lambda n, xr, zr: pltpu.VMEM((n, 6, 4, xr, TILE), F32)),
        per_class(lambda n, xr, zr: pltpu.VMEM((n, 8, xr, TILE), F32)),
        per_class(lambda n, xr, zr: pltpu.VMEM((n, 8, NX, zr, TILE), F32)),
        per_class(lambda n, xr, zr: pltpu.VMEM((n, 6, zr, TILE), F32)),
    ]
    scratch += [
        pltpu.VMEM((NX, NZ, 8, 128), F32),
        pltpu.VMEM((NX - 1, NZ, 8, 128), F32),
        pltpu.VMEM((NZ, 8, 128), F32),
        pltpu.VMEM((NZ - 1, 8, 128), F32),
        pltpu.VMEM((PATCH, 128), F32),
        pltpu.VMEM((64, COLS + 2 * PAD), F32),
        pltpu.VMEM((NT, NB, 16, TILE), F32),
        pltpu.VMEM((NT, NB - 1, 16, TILE), F32),
    ]
    dma = pltpu.SemaphoreType.DMA
    scratch += [
        dma((8,)), dma((2, NT)), dma((NT,)), dma((2,)), dma((NT,)), dma((NT,)),
        per_class(lambda n, xr, zr: dma((n, MESSAGES))),
        per_class(lambda n, xr, zr: dma((n, MESSAGES))),
        dma((NX - 1 + NZ - 1,)), dma((NX - 1 + NZ - 1,)),
        dma((NT, NB - 1)), dma((NT, NB - 1)),
    ]
    coadd, detection = pl.pallas_call(
        kernel,
        out_shape=(
            jax.ShapeDtypeStruct((1, PATCH, COLS), F32),
            jax.ShapeDtypeStruct((SLAB, COLS), F32),
        ),
        in_specs=[anywhere] * 9,
        out_specs=(anywhere, anywhere),
        scratch_shapes=scratch,
        compiler_params=pltpu.CompilerParams(
            collective_id=0, has_side_effects=True, vmem_limit_bytes=60 << 20
        ),
        cost_estimate=pl.CostEstimate(
            flops=20_000_000_000, bytes_accessed=5_000_000, transcendentals=0
        ),
    )(images, row_kernel, col_kernel, *lists, drt, dct, bw)
    vmem = pl.BlockSpec(memory_space=pltpu.VMEM)
    return pl.pallas_call(
        hand_over,
        out_shape=(
            jax.ShapeDtypeStruct((1, PATCH, COLS), F32),
            jax.ShapeDtypeStruct((SLAB, COLS), F32),
        ),
        in_specs=[vmem] * 2,
        out_specs=(vmem, vmem),
    )(coadd, detection)


def solution(mesh):
    placed = (P("band", "visit", None),) * 6 + (P(), P(), P())
    return jax.shard_map(
        on_device,
        mesh=mesh,
        in_specs=placed,
        out_specs=(P("band", "visit", None), P(("visit", "band"), None)),
        check_vma=False,
    )
```
